128 devices in a mesh: blk: 8 (over y_lo, z), env: 16 (over y_hi, x, core).
Axes of the slice: x: 4, y: 4 (y_hi: 2, y_lo: 2; y = y_hi * 2 + y_lo), z: 4, core: 2. Of those that a mesh axis runs over, the one named last changes fastest.
Arguments:
- psi: float32 [64, 512, 512], P('blk'), may hold values from -6 to 6
- left_env: float32 [32, 16, 512, 512], P('env', 'blk'), may hold values from -0.25 to 0.25
- right_env: float32 [32, 16, 512, 512], P('env', 'blk'), may hold values from -0.046875 to 0.046875
- source: int32 [64, 32], P('blk', 'env'), may hold values from 0 to 63, as said below
- left_sector: int32 [64, 32], P('blk', 'env'), may hold values from 0 to 15, as said below
- right_sector: int32 [64, 32], P('blk', 'env'), may hold values from 0 to 15, as said below
- live: int32 [64, 32], P('blk', 'env'), may hold values from 0 to 1
Outputs:
- sigma: float32 [64, 512, 512], P('blk', 'env')
The draws below stay inside these ranges and needn't reach their ends.
Inputs may be any that keep to these rules, and one draw needn't show every extreme that they name: source[b, k] - b taken modulo 64 is -1, 0 or 1; both -1 and 1 occur. left_sector[b, k] // 2 == b // 8. right_sector[b, k] // 2 == b // 8.
All inputs are finite; a program needn't handle non-finite values.
Results may differ from the reference program's by a relative error of at most 0.0001.
Values sent between devices are 32-bit elements; how exact they have to be, the bound alone decides.
A program may use at most 192 MiB of HBM per device.

```python
import jax
import jax.numpy as jnp
from jax import lax

BS = 512
BLK_DEV = 8
NS_DEV = 2
NB = 64
K = 32
NS = 16


def draw_source(key, part):
    key = jax.random.fold_in(key, 11)
    key_off, key_row = jax.random.split(key)
    offset = jax.random.randint(key_off, (NB, K), -1, 2)
    row = jax.random.randint(key_row, (), 0, NB)
    offset = offset.at[row, 0].set(-1).at[row, 1].set(1)
    blocks = jnp.arange(NB, dtype=jnp.int32)[:, None]
    return ((blocks + offset + NB) % NB).astype(jnp.int32)


def sector_table(key):
    owner = jnp.arange(NB, dtype=jnp.int32)[:, None] // BLK_DEV
    pick = jax.random.randint(key, (NB, K), 0, NS_DEV)
    return (owner * NS_DEV + pick).astype(jnp.int32)


def draw_left_sector(key, part):
    key = jax.random.fold_in(key, 12)
    return sector_table(key)


def draw_right_sector(key, part):
    key = jax.random.fold_in(key, 13)
    return sector_table(key)


def draw_live(key, part):
    key = jax.random.fold_in(key, 14)
    key_level, key_pick = jax.random.split(key)
    level = jax.random.randint(key_level, (NB // BLK_DEV,), 1, 5)
    owner = jnp.arange(NB, dtype=jnp.int32) // BLK_DEV
    pick = jax.random.randint(key_pick, (NB, K), 0, 4)
    return (pick < level[owner][:, None]).astype(jnp.int32)


def block_scale(stream_key, shape, cuts, smallest, top_value):
    level = 1.0
    for position, shards_of in cuts:
        heights = jax.random.uniform(jax.random.fold_in(jax.random.fold_in(stream_key, 6), position), (shards_of,), jnp.float32, smallest / len(cuts), top_value / len(cuts))
        level = level * jnp.repeat(jnp.exp(heights), shape[position] // shards_of).reshape((-1,) + (1,) * (len(shape) - 1 - position))
    return level


def centred(rng, extent, scale, most, shards=(), kind=jnp.bfloat16):
    level = block_scale(rng, extent, shards, -0.22, 0.18) if shards else 1.0
    entries = jax.random.normal(rng, extent, jnp.float32) * scale * level
    return jnp.minimum(jnp.maximum(entries, -most), most).astype(kind)


def setup_inputs(seed: int = 0) -> dict:
    streams_of = jax.random.split(jax.random.key(seed), 8)
    psi = centred(streams_of[0], (NB, BS, BS), 1.0, 6.0, ((0, 8),), jnp.float32)
    left_env = centred(streams_of[1], (K, NS, BS, BS), BS ** -0.5, 0.25, ((0, 16), (1, 8)), jnp.float32)
    right_env = centred(streams_of[2], (K, NS, BS, BS), (BS * K) ** -0.5, 0.046875, ((0, 16), (1, 8)), jnp.float32)
    source = draw_source(jax.random.fold_in(streams_of[7], 71), 0)
    left_sector = draw_left_sector(jax.random.fold_in(streams_of[7], 71), 0)
    right_sector = draw_right_sector(jax.random.fold_in(streams_of[7], 71), 0)
    live = draw_live(jax.random.fold_in(streams_of[7], 71), 0)
    return dict(psi=psi, left_env=left_env, right_env=right_env, source=source, left_sector=left_sector, right_sector=right_sector, live=live)


def reference(psi, left_env, right_env, source, left_sector, right_sector, live):
    def one_block(index):
        def channel(total, k):
            left = left_env[k, left_sector[index, k]]
            middle = psi[source[index, k]]
            right = right_env[k, right_sector[index, k]]
            inner = jnp.dot(left, middle, precision=lax.Precision.HIGHEST, preferred_element_type=jnp.float32)
            term = jnp.dot(inner, right, precision=lax.Precision.HIGHEST, preferred_element_type=jnp.float32)
            return total + live[index, k].astype(jnp.float32) * term, None

        total, _ = lax.scan(channel, jnp.zeros((BS, BS), jnp.float32), jnp.arange(K, dtype=jnp.int32))
        return total

    return lax.map(one_block, jnp.arange(NB, dtype=jnp.int32))
```

```python
import functools

import jax
import jax.numpy as jnp
from jax import lax
from jax.experimental import pallas as pl
from jax.experimental.pallas import tpu as pltpu
from jax.sharding import PartitionSpec as P

MESH = pl.DeviceIdType.MESH
BF16 = jnp.bfloat16
F32 = jnp.float32

WIDTH = 512
BLOCKS = 8
STRIP = 32
HALF = 256
HALO_HI, HALO_LO = 8, 9
ORDER = ((0, 0), (1, 0), (0, 1), (1, 3), (0, 2), (1, 1), (1, 2), (0, 3))
CORE, XA1, XA2, YA, YB, XB1, XB2, KINDS = 0, 1, 3, 5, 6, 7, 9, 11


def split(x):
    hi = x.astype(BF16)
    return hi, (x - hi.astype(F32)).astype(BF16)


def dot3(a_hi, a_lo, b_hi, b_lo):
    dot = functools.partial(jnp.dot, preferred_element_type=F32)
    return dot(a_hi, b_hi) + dot(a_hi, b_lo) + dot(a_lo, b_hi)


def kernel(
    source, left_sector, right_sector, live, psi, left, right, out,
    stage, land, p_hi, p_lo, l_hi, l_lo, r_hi, r_lo, cland, sa, sb, xa1, xa2, ya, yb, xb1, xb2, done,
    psi_sem, left_sem, right_sem, halo_send, halo_recv, pass_send, pass_recv, send, recv, out_sem,
):
    blk, env = lax.axis_index("blk"), lax.axis_index("env")
    core, x, y_hi = env % 2, (env // 2) % 4, env // 8

    def env_at(y, xx, c):
        return (y * 4 + xx) * 2 + c

    sibling = (blk, env_at(y_hi, x, 1 - core))
    x_up = (blk, env_at(y_hi, (x + 1) % 4, core))
    x_down = (blk, env_at(y_hi, (x + 3) % 4, core))
    y_other = (blk, env_at(1 - y_hi, x, core))
    blk_up = ((blk + 1) % 8, env)
    blk_down = ((blk + 7) % 8, env)

    def load(what, src, dst, sem):
        return pltpu.make_async_copy(src, dst, sem)

    def left_load(m):
        return load("l", left.at[m], stage.at[m], left_sem.at[m])

    def right_load(m):
        return load("r", right.at[m], stage.at[4 + m], right_sem.at[m])

    def psi_load(j):
        return load("p", psi.at[j], land.at[j], psi_sem.at[j])

    for m in range(4):
        left_load(m).start()
    for j in (0, 1, 2):
        psi_load(j).start()
    for m in range(4):
        right_load(m).start()
    for j in (7, 3, 4, 5, 6):
        psi_load(j).start()

    barrier = pltpu.get_barrier_semaphore()
    for peer in (sibling, x_up, x_down, y_other, blk_up, blk_down):
        pl.semaphore_signal(barrier, inc=1, device_id=peer, device_id_type=MESH)
    pl.semaphore_wait(barrier, 6)

    def remote(src, dst, s, r, peer):
        return pltpu.make_async_remote_copy(
            src_ref=src, dst_ref=dst, send_sem=s, recv_sem=r, device_id=peer, device_id_type=MESH
        )

    my_half = pl.ds(core * HALF, HALF)

    def halo(n):
        mine, theirs, peer = ((0, HALO_HI, blk_down), (7, HALO_LO, blk_up))[n]
        return remote(
            land.at[mine, my_half], land.at[theirs, my_half], halo_send.at[n], halo_recv.at[n], peer
        )

    def halo_pass(n):
        item = (HALO_HI, HALO_LO)[n]
        return remote(
            land.at[item, my_half], land.at[item, my_half], pass_send.at[n], pass_recv.at[n], sibling
        )

    def convert(j):
        hi, lo = split(land[j])
        p_hi[j] = hi
        p_lo[j] = lo

    def convert_left(m):
        left_load(m).wait()
        for half in range(2):
            for s, (dy, dx) in enumerate(ORDER):
                owner = env_at((y_hi + dy) % 2, (x + dx) % 4, (core + 1 + half) % 2)
                hi, lo = split(stage[m, pl.ds(owner * STRIP, STRIP)])
                rows = pl.ds((half * 8 + s) * STRIP, STRIP)
                l_hi[m, rows] = hi
                l_lo[m, rows] = lo

    def convert_right(m):
        right_load(m).wait()
        hi, lo = split(stage[4 + m])
        r_hi[m] = hi
        r_lo[m] = lo

    for m in range(4):
        convert_left(m)
    psi_load(0).wait()
    halo(0).start()
    convert(0)
    for j in (1, 2):
        psi_load(j).wait()
        convert(j)
    for m in range(4):
        convert_right(m)
    psi_load(7).wait()
    halo(1).start()

    def compute(i):
        b = (i + 1) % 8
        glob = blk * BLOCKS + b
        total = None
        for k in range(2):
            offset = jnp.minimum((source[b, k] - glob + 65) % 64, 2) - 1
            item = b + offset
            item = jnp.where(item < 0, HALO_LO, item)
            lm = left_sector[b, k] % 2 + 2 * k
            rm = right_sector[b, k] % 2 + 2 * k
            weight = live[b, k].astype(F32)
            inner = dot3(l_hi[lm], l_lo[lm], p_hi[item], p_lo[item])
            hi, lo = split(inner * weight)
            term = dot3(hi, lo, r_hi[rm], r_lo[rm])
            total = term if total is None else total + term
        stage[i] = total

    def core_copy(i):
        return remote(
            stage.at[i, pl.ds(0, HALF)], cland.at[i], send.at[i, CORE], recv.at[i, CORE], sibling
        )

    def xa1_copy(i, d):
        return remote(
            sa.at[i, pl.ds(4 + 2 * d, 2)], xa1.at[i, d], send.at[i, XA1 + d], recv.at[i, XA1 + d],
            (x_up, x_down)[d],
        )

    def xa2_copy(i, d):
        return remote(
            sa.at[i, 2 + d], xa2.at[i, d], send.at[i, XA2 + d], recv.at[i, XA2 + d], (x_up, x_down)[d]
        )

    def ya_copy(i):
        return remote(sa.at[i, 1], ya.at[i], send.at[i, YA], recv.at[i, YA], y_other)

    def yb_copy(i):
        return remote(sb.at[i, pl.ds(8, 8)], yb.at[i], send.at[i, YB], recv.at[i, YB], y_other)

    def xb1_copy(i, d):
        return remote(
            sb.at[i, pl.ds(4 + 2 * d, 2)], xb1.at[i, d], send.at[i, XB1 + d], recv.at[i, XB1 + d],
            (x_up, x_down)[d],
        )

    def xb2_copy(i, d):
        return remote(
            sb.at[i, 2 + d], xb2.at[i, d], send.at[i, XB2 + d], recv.at[i, XB2 + d], (x_up, x_down)[d]
        )

    def out_copy(i):
        return pltpu.make_async_copy(done.at[i], out.at[(i + 1) % 8], out_sem.at[i])

    def step1(i):
        core_copy(i).wait_recv()
        for s, (dy, dx) in enumerate(ORDER):
            rows = pl.ds(s * STRIP, STRIP)
            strip = stage[i, pl.ds(HALF + s * STRIP, STRIP)] + cland[i, rows]
            sa[i, s] = strip[:, :HALF]
            for h in range(2):
                where = {(0, 0): 0, (0, 1): 1, (1, 0): 2, (1, 1): 5, (2, 0): 4, (2, 1): 6, (3, 0): 7, (3, 1): 3}
                sb[i, 8 * dy + where[dx, h]] = strip[h * 16:(h + 1) * 16, HALF:]
        yb_copy(i).start()
        xa1_copy(i, 0).start()
        xa1_copy(i, 1).start()

    def step2(i):
        for d in range(2):
            xa1_copy(i, d).wait_recv()
            sa[i, 2 + d] += xa1[i, d, 0]
            xa2_copy(i, d).start()
        yb_copy(i).wait_recv()
        sb[i, pl.ds(0, 8)] += yb[i]
        xb1_copy(i, 0).start()
        xb1_copy(i, 1).start()

    def step3(i):
        for d in range(2):
            xa2_copy(i, d).wait_recv()
        sa[i, 1] += xa1[i, 0, 1] + xa2[i, 1]
        ya_copy(i).start()
        for d in range(2):
            xb1_copy(i, d).wait_recv()
            sb[i, 2 + d] += xb1[i, d, 0]
            xb2_copy(i, d).start()

    def step4(i):
        for d in range(2):
            xb2_copy(i, d).wait_recv()
        done[i, pl.ds(0, 16), pl.ds(HALF, HALF)] = sb[i, 0] + xb2[i, 0] + xb1[i, 1, 1]
        done[i, pl.ds(16, 16), pl.ds(HALF, HALF)] = sb[i, 1] + xb1[i, 0, 1] + xb2[i, 1]
        ya_copy(i).wait_recv()
        done[i, :, pl.ds(0, HALF)] = (sa[i, 0] + xa2[i, 0] + xa1[i, 1, 1]) + ya[i]
        out_copy(i).start()

    steps = (step1, step2, step3, step4)

    def iteration(i, carry):
        item = jnp.minimum(i + 3, 9)

        @pl.when(i < 4)
        def _():
            psi_load(i + 3).wait()

        @pl.when(i == 3)
        def _():
            for n in range(2):
                halo(n).wait_recv()
                halo_pass(n).start()

        @pl.when(i == 5)
        def _():
            halo_pass(0).wait_recv()

        @pl.when(i == 6)
        def _():
            halo_pass(1).wait_recv()

        convert(item)
        compute(i)
        core_copy(i).start()
        for n, step in enumerate(steps):
            @pl.when(i > n)
            def _():
                step(i - 1 - n)
        return carry

    lax.fori_loop(0, BLOCKS, iteration, 0)
    for late in range(4):
        for n, step in enumerate(steps):
            if n >= late:
                step(7 + late - n)

    for n in range(2):
        halo(n).wait_send()
        halo_pass(n).wait_send()

    def finish(i, carry):
        core_copy(i).wait_send()
        for d in range(2):
            xa1_copy(i, d).wait_send()
            xa2_copy(i, d).wait_send()
            xb1_copy(i, d).wait_send()
            xb2_copy(i, d).wait_send()
        ya_copy(i).wait_send()
        yb_copy(i).wait_send()
        out_copy(i).wait()
        return carry

    lax.fori_loop(0, BLOCKS, finish, 0)


def body(psi, left_env, right_env, source, left_sector, right_sector, live):
    vmem = pltpu.VMEM
    dma = pltpu.SemaphoreType.DMA
    square = (WIDTH, WIDTH)
    smem = pl.BlockSpec(memory_space=pltpu.SMEM)
    hbm = pl.BlockSpec(memory_space=pl.ANY)
    return pl.pallas_call(
        kernel,
        out_shape=jax.ShapeDtypeStruct((BLOCKS, STRIP, WIDTH), F32),
        in_specs=[smem] * 4 + [hbm] * 3,
        out_specs=hbm,
        scratch_shapes=[
            vmem((8, *square), F32),
            vmem((10, *square), F32),
            vmem((10, *square), BF16),
            vmem((10, *square), BF16),
            vmem((4, *square), BF16),
            vmem((4, *square), BF16),
            vmem((4, *square), BF16),
            vmem((4, *square), BF16),
            vmem((8, HALF, WIDTH), F32),
            vmem((8, 8, STRIP, HALF), F32),
            vmem((8, 16, 16, HALF), F32),
            vmem((8, 2, 2, STRIP, HALF), F32),
            vmem((8, 2, STRIP, HALF), F32),
            vmem((8, STRIP, HALF), F32),
            vmem((8, 8, 16, HALF), F32),
            vmem((8, 2, 2, 16, HALF), F32),
            vmem((8, 2, 16, HALF), F32),
            vmem((8, STRIP, WIDTH), F32),
            dma((8,)), dma((4,)), dma((4,)),
            dma((2,)), dma((2,)), dma((2,)), dma((2,)),
            dma((8, KINDS)), dma((8, KINDS)), dma((8,)),
        ],
        compiler_params=pltpu.CompilerParams(
            collective_id=0, has_side_effects=True, vmem_limit_bytes=60 * 2**20
        ),
    )(
        source, left_sector, right_sector, live, psi,
        left_env.reshape(4, *square), right_env.reshape(4, *square),
    )


def solution(mesh):
    placed = (
        P("blk", None, None),
        P("env", "blk", None, None),
        P("env", "blk", None, None),
        P("blk", "env"),
        P("blk", "env"),
        P("blk", "env"),
        P("blk", "env"),
    )
    return jax.shard_map(
        body, mesh=mesh, in_specs=placed, out_specs=P("blk", "env", None), check_vma=False
    )
```

```python
import functools

import jax
import jax.numpy as jnp
from jax import lax
from jax.experimental import pallas as pl
from jax.experimental.pallas import tpu as pltpu
from jax.sharding import PartitionSpec as P

MESH = pl.DeviceIdType.MESH
BF16 = jnp.bfloat16
F32 = jnp.float32

WIDTH = 512
BLOCKS = 8
STRIP = 32
HALF = 256
CUT = 384
REST = WIDTH - CUT
OFFSETS = (2, 6, 10, 14)
HALO_HI, HALO_LO = 8, 9
ORDER = ((0, 0), (1, 0), (0, 1), (1, 3), (0, 2), (1, 1), (1, 2), (0, 3))
CORE, XA1, XA2, YA, YB, XB1, XB2, KINDS = 0, 1, 3, 5, 6, 7, 9, 11


def split(x):
    hi = x.astype(BF16)
    return hi, (x - hi.astype(F32)).astype(BF16)


def dot3(a_hi, a_lo, b_hi, b_lo):
    dot = functools.partial(jnp.dot, preferred_element_type=F32)
    return dot(a_hi, b_hi) + dot(a_hi, b_lo) + dot(a_lo, b_hi)


def kernel(
    source, left_sector, right_sector, live, psi, left, right, out,
    table, stage, land, p_hi, p_lo, l_hi, l_lo, r_hi, r_lo, i_hi, i_lo,
    cland, sa, sb, xa1, xa2, ya, yb, xb1, xb2, done,
    table_sem, psi_sem, left_sem, right_sem, halo_send, halo_recv, pass_send, pass_recv, send, recv,
    out_sem,
):
    blk, env = lax.axis_index("blk"), lax.axis_index("env")
    core, x, y_hi = env % 2, (env // 2) % 4, env // 8

    def env_at(y, xx, c):
        return (y * 4 + xx) * 2 + c

    sibling = (blk, env_at(y_hi, x, 1 - core))
    x_up = (blk, env_at(y_hi, (x + 1) % 4, core))
    x_down = (blk, env_at(y_hi, (x + 3) % 4, core))
    y_other = (blk, env_at(1 - y_hi, x, core))
    blk_up = ((blk + 1) % 8, env)
    blk_down = ((blk + 7) % 8, env)

    def left_load(m):
        return pltpu.make_async_copy(left.at[m], stage.at[m], left_sem.at[m])

    def right_load(m):
        return pltpu.make_async_copy(right.at[m], stage.at[4 + m], right_sem.at[m])

    def psi_load(j):
        return pltpu.make_async_copy(psi.at[j], land.at[j], psi_sem.at[j])

    table_loads = [
        pltpu.make_async_copy(ref, table.at[n], table_sem.at[n])
        for n, ref in enumerate((source, left_sector, right_sector, live))
    ]
    for copy in table_loads:
        copy.start()
    for m in (0, 1):
        left_load(m).start()
    for j in (0, 1, 2):
        psi_load(j).start()
    for m in (2, 3):
        left_load(m).start()
    for m in range(4):
        right_load(m).start()
    for j in (7, 3, 4, 5, 6):
        psi_load(j).start()

    barrier = pltpu.get_barrier_semaphore()
    for peer in (sibling, x_up, x_down, y_other, blk_up, blk_down):
        pl.semaphore_signal(barrier, inc=1, device_id=peer, device_id_type=MESH)

    def remote(src, dst, s, r, peer):
        return pltpu.make_async_remote_copy(
            src_ref=src, dst_ref=dst, send_sem=s, recv_sem=r, device_id=peer, device_id_type=MESH
        )

    my_half = pl.ds(core * HALF, HALF)

    def halo(n):
        mine, theirs, peer = ((0, HALO_HI, blk_down), (7, HALO_LO, blk_up))[n]
        return remote(
            psi.at[mine, my_half], land.at[theirs, my_half], halo_send.at[n], halo_recv.at[n], peer
        )

    def halo_pass(n):
        item = (HALO_HI, HALO_LO)[n]
        return remote(
            land.at[item, my_half], land.at[item, my_half], pass_send.at[n], pass_recv.at[n], sibling
        )

    def convert(j):
        hi, lo = split(land[j])
        p_hi[j] = hi
        p_lo[j] = lo

    def convert_left(m):
        left_load(m).wait()
        for half in range(2):
            for s, (dy, dx) in enumerate(ORDER):
                owner = env_at((y_hi + dy) % 2, (x + dx) % 4, (core + 1 + half) % 2)
                hi, lo = split(stage[m, pl.ds(owner * STRIP, STRIP)])
                rows = pl.ds((half * 8 + s) * STRIP, STRIP)
                l_hi[m, rows] = hi
                l_lo[m, rows] = lo

    def convert_right(m):
        right_load(m).wait()
        hi, lo = split(stage[4 + m])
        r_hi[m] = hi
        r_lo[m] = lo

    def first(i, k):
        b = (i + 1) % 8
        offset = jnp.minimum((table[0, k, b] - (blk * BLOCKS + b) + 65) % 64, 2) - 1
        item = b + offset
        item = jnp.where(item < 0, HALO_LO, item)
        lm = table[1, k, b] % 2 + 2 * k
        weight = table[3, k, b].astype(F32)
        inner = dot3(l_hi[lm], l_lo[lm], p_hi[item], p_lo[item])
        hi, lo = split(inner * weight)
        i_hi[k] = hi
        i_lo[k] = lo

    def second(i):
        b = (i + 1) % 8
        total = None
        for k in range(2):
            rm = table[2, k, b] % 2 + 2 * k
            term = dot3(i_hi[k], i_lo[k], r_hi[rm], r_lo[rm])
            total = term if total is None else total + term
        stage[i] = total

    def core_copy(i):
        return remote(
            stage.at[i, pl.ds(0, HALF)], cland.at[i], send.at[i, CORE], recv.at[i, CORE], sibling
        )

    def xa1_copy(i, d):
        return remote(
            sa.at[i, pl.ds(4 + 2 * d, 2)], xa1.at[i, d], send.at[i, XA1 + d], recv.at[i, XA1 + d],
            (x_up, x_down)[d],
        )

    def xa2_copy(i, d):
        return remote(
            sa.at[i, 2 + d], xa2.at[i, d], send.at[i, XA2 + d], recv.at[i, XA2 + d], (x_up, x_down)[d]
        )

    def ya_copy(i):
        return remote(sa.at[i, 1], ya.at[i], send.at[i, YA], recv.at[i, YA], y_other)

    def yb_copy(i):
        return remote(sb.at[i, pl.ds(8, 8)], yb.at[i], send.at[i, YB], recv.at[i, YB], y_other)

    def xb1_copy(i, d):
        return remote(
            sb.at[i, pl.ds(4 + 2 * d, 2)], xb1.at[i, d], send.at[i, XB1 + d], recv.at[i, XB1 + d],
            (x_up, x_down)[d],
        )

    def xb2_copy(i, d):
        return remote(
            sb.at[i, 2 + d], xb2.at[i, d], send.at[i, XB2 + d], recv.at[i, XB2 + d], (x_up, x_down)[d]
        )

    def out_copy(i):
        return pltpu.make_async_copy(done.at[i], out.at[(i + 1) % 8], out_sem.at[i])

    def step1(i):
        core_copy(i).wait_recv()
        for s, (dy, dx) in enumerate(ORDER):
            rows = pl.ds(s * STRIP, STRIP)
            strip = stage[i, pl.ds(HALF + s * STRIP, STRIP)] + cland[i, rows]
            sa[i, s] = strip[:, :CUT]
            for h in range(2):
                where = {(0, 0): 0, (0, 1): 1, (1, 0): 2, (1, 1): 5, (2, 0): 4, (2, 1): 6, (3, 0): 7, (3, 1): 3}
                sb[i, 8 * dy + where[dx, h]] = strip[h * 16:(h + 1) * 16, CUT:]
        yb_copy(i).start()
        xa1_copy(i, 0).start()
        xa1_copy(i, 1).start()

    def step2(i):
        for d in range(2):
            xa1_copy(i, d).wait_recv()
            sa[i, 2 + d] += xa1[i, d, 0]
            xa2_copy(i, d).start()
        yb_copy(i).wait_recv()
        sb[i, pl.ds(0, 8)] += yb[i]
        xb1_copy(i, 0).start()
        xb1_copy(i, 1).start()

    def step3(i):
        for d in range(2):
            xa2_copy(i, d).wait_recv()
        sa[i, 1] += xa1[i, 0, 1] + xa2[i, 1]
        ya_copy(i).start()
        for d in range(2):
            xb1_copy(i, d).wait_recv()
            sb[i, 2 + d] += xb1[i, d, 0]
            xb2_copy(i, d).start()

    def step4(i):
        for d in range(2):
            xb2_copy(i, d).wait_recv()
        done[i, pl.ds(0, 16), pl.ds(CUT, REST)] = sb[i, 0] + xb2[i, 0] + xb1[i, 1, 1]
        done[i, pl.ds(16, 16), pl.ds(CUT, REST)] = sb[i, 1] + xb1[i, 0, 1] + xb2[i, 1]
        ya_copy(i).wait_recv()
        done[i, :, pl.ds(0, CUT)] = (sa[i, 0] + xa2[i, 0] + xa1[i, 1, 1]) + ya[i]
        out_copy(i).start()

    steps = (step1, step2, step3, step4)

    def run_steps(i, slot):
        for step, offset in zip(steps, OFFSETS):
            if offset % 2 == slot:
                ago = offset // 2
                if isinstance(i, int):
                    if i >= ago:
                        step(i - ago)
                else:
                    @pl.when(i >= ago)
                    def _():
                        step(i - ago)

    for copy in table_loads:
        copy.wait()
    convert_left(0)
    convert_left(1)
    for j in (0, 1, 2):
        psi_load(j).wait()
        convert(j)
    first(0, 0)
    convert_left(2)
    convert_left(3)
    first(0, 1)
    pl.semaphore_wait(barrier, 6)
    halo(0).start()
    halo(1).start()
    for m in range(4):
        convert_right(m)
    second(0)
    core_copy(0).start()
    psi_load(3).wait()
    convert(3)

    def iteration(i, carry):
        first(i, 0)
        first(i, 1)
        run_steps(i, 0)

        @pl.when(i == 4)
        def _():
            for n in range(2):
                halo(n).wait_recv()
                halo_pass(n).start()

        second(i)
        core_copy(i).start()

        @pl.when(i < 5)
        def _():
            psi_load(i + 3).wait()

        @pl.when(i == 5)
        def _():
            halo_pass(0).wait_recv()

        @pl.when(i == 6)
        def _():
            halo_pass(1).wait_recv()

        convert(jnp.minimum(i + 3, 9))
        run_steps(i, 1)
        return carry

    lax.fori_loop(1, BLOCKS, iteration, 0)
    late = [(2 * i + off, n, i) for i in range(BLOCKS) for n, off in enumerate(OFFSETS) if 2 * i + off > 15]
    for _, n, i in sorted(late):
        steps[n](i)

    for n in range(2):
        halo(n).wait_send()
        halo_pass(n).wait_send()

    def finish(i, carry):
        core_copy(i).wait_send()
        for d in range(2):
            xa1_copy(i, d).wait_send()
            xa2_copy(i, d).wait_send()
            xb1_copy(i, d).wait_send()
            xb2_copy(i, d).wait_send()
        ya_copy(i).wait_send()
        yb_copy(i).wait_send()
        out_copy(i).wait()
        return carry

    lax.fori_loop(0, BLOCKS, finish, 0)


def body(psi, left_env, right_env, source, left_sector, right_sector, live):
    vmem = pltpu.VMEM
    dma = pltpu.SemaphoreType.DMA
    square = (WIDTH, WIDTH)
    hbm = pl.BlockSpec(memory_space=pl.ANY)
    return pl.pallas_call(
        kernel,
        out_shape=jax.ShapeDtypeStruct((BLOCKS, STRIP, WIDTH), F32),
        in_specs=[hbm] * 7,
        out_specs=hbm,
        scratch_shapes=[
            pltpu.SMEM((4, 2, BLOCKS), jnp.int32),
            vmem((8, *square), F32),
            vmem((10, *square), F32),
            vmem((10, *square), BF16),
            vmem((10, *square), BF16),
            vmem((4, *square), BF16),
            vmem((4, *square), BF16),
            vmem((4, *square), BF16),
            vmem((4, *square), BF16),
            vmem((2, *square), BF16),
            vmem((2, *square), BF16),
            vmem((8, HALF, WIDTH), F32),
            vmem((8, 8, STRIP, CUT), F32),
            vmem((8, 16, 16, REST), F32),
            vmem((8, 2, 2, STRIP, CUT), F32),
            vmem((8, 2, STRIP, CUT), F32),
            vmem((8, STRIP, CUT), F32),
            vmem((8, 8, 16, REST), F32),
            vmem((8, 2, 2, 16, REST), F32),
            vmem((8, 2, 16, REST), F32),
            vmem((8, STRIP, WIDTH), F32),
            dma((4,)), dma((8,)), dma((4,)), dma((4,)),
            dma((2,)), dma((2,)), dma((2,)), dma((2,)),
            dma((8, KINDS)), dma((8, KINDS)),
            dma((8,)),
        ],
        compiler_params=pltpu.CompilerParams(
            collective_id=0, has_side_effects=True, vmem_limit_bytes=60 * 2**20
        ),
    )(
        source.T, left_sector.T, right_sector.T, live.T, psi,
        left_env.reshape(4, *square), right_env.reshape(4, *square),
    )


def solution(mesh):
    placed = (
        P("blk", None, None),
        P("env", "blk", None, None),
        P("env", "blk", None, None),
        P("blk", "env"),
        P("blk", "env"),
        P("blk", "env"),
        P("blk", "env"),
    )
    return jax.shard_map(
        body, mesh=mesh, in_specs=placed, out_specs=P("blk", "env", None), check_vma=False
    )
```

```python
import functools

import jax
import jax.numpy as jnp
from jax import lax
from jax.experimental import pallas as pl
from jax.experimental.pallas import tpu as pltpu
from jax.sharding import PartitionSpec as P

MESH = pl.DeviceIdType.MESH
BF16 = jnp.bfloat16
F32 = jnp.float32

WIDTH = 512
BLOCKS = 8
STRIP = 32
HALF = 256
CUT = 384
REST = WIDTH - CUT
OFFSETS = (2, 7, 11, 15)
HALO_HI, HALO_LO = 8, 9
ORDER = ((0, 0), (1, 0), (0, 1), (1, 3), (0, 2), (1, 1), (1, 2), (0, 3))
CORE, XA1, XA2, YA, YB, XB1, XB2, KINDS = 0, 1, 3, 5, 6, 7, 9, 11


def split(x):
    hi = x.astype(BF16)
    return hi, (x - hi.astype(F32)).astype(BF16)


def dot3(a_hi, a_lo, b_hi, b_lo):
    dot = functools.partial(jnp.dot, preferred_element_type=F32)
    return dot(a_hi, b_hi) + dot(a_hi, b_lo) + dot(a_lo, b_hi)


def kernel(
    source, left_sector, right_sector, live, psi, left, right, out,
    table, stage, land, p_hi, p_lo, l_hi, l_lo, r_hi, r_lo, i_hi, i_lo,
    cland, sa, sb, xa1, xa2, ya, yb, xb1, xb2, done,
    table_sem, psi_sem, left_sem, right_sem, halo_send, halo_recv, pass_send, pass_recv, send, recv,
    out_sem,
):
    blk, env = lax.axis_index("blk"), lax.axis_index("env")
    core, x, y_hi = env % 2, (env // 2) % 4, env // 8

    def env_at(y, xx, c):
        return (y * 4 + xx) * 2 + c

    sibling = (blk, env_at(y_hi, x, 1 - core))
    x_up = (blk, env_at(y_hi, (x + 1) % 4, core))
    x_down = (blk, env_at(y_hi, (x + 3) % 4, core))
    y_other = (blk, env_at(1 - y_hi, x, core))
    blk_up = ((blk + 1) % 8, env)
    blk_down = ((blk + 7) % 8, env)

    def left_load(m):
        return pltpu.make_async_copy(left.at[m], stage.at[m], left_sem.at[m])

    def right_load(m):
        return pltpu.make_async_copy(right.at[m], stage.at[4 + m], right_sem.at[m])

    def psi_load(j):
        return pltpu.make_async_copy(psi.at[j], land.at[j], psi_sem.at[j])

    table_loads = [
        pltpu.make_async_copy(ref, table.at[n], table_sem.at[n])
        for n, ref in enumerate((source, left_sector, right_sector, live))
    ]
    for copy in table_loads:
        copy.start()
    for m in (0, 1):
        left_load(m).start()
    for j in (0, 1, 2):
        psi_load(j).start()
    for m in (2, 3):
        left_load(m).start()
    for m in range(4):
        right_load(m).start()
    for j in (7, 3, 4, 5, 6):
        psi_load(j).start()

    barrier = pltpu.get_barrier_semaphore()
    for peer in (sibling, x_up, x_down, y_other, blk_up, blk_down):
        pl.semaphore_signal(barrier, inc=1, device_id=peer, device_id_type=MESH)

    def remote(src, dst, s, r, peer):
        return pltpu.make_async_remote_copy(
            src_ref=src, dst_ref=dst, send_sem=s, recv_sem=r, device_id=peer, device_id_type=MESH
        )

    my_half = pl.ds(core * HALF, HALF)

    def halo(n):
        mine, theirs, peer = ((0, HALO_HI, blk_down), (7, HALO_LO, blk_up))[n]
        return remote(
            psi.at[mine, my_half], land.at[theirs, my_half], halo_send.at[n], halo_recv.at[n], peer
        )

    def halo_pass(n):
        item = (HALO_HI, HALO_LO)[n]
        return remote(
            land.at[item, my_half], land.at[item, my_half], pass_send.at[n], pass_recv.at[n], sibling
        )

    def convert(j):
        hi, lo = split(land[j])
        p_hi[j] = hi
        p_lo[j] = lo

    def convert_left(m):
        left_load(m).wait()
        for half in range(2):
            for s, (dy, dx) in enumerate(ORDER):
                owner = env_at((y_hi + dy) % 2, (x + dx) % 4, (core + 1 + half) % 2)
                hi, lo = split(stage[m, pl.ds(owner * STRIP, STRIP)])
                rows = pl.ds((half * 8 + s) * STRIP, STRIP)
                l_hi[m, rows] = hi
                l_lo[m, rows] = lo

    def convert_right(m):
        right_load(m).wait()
        hi, lo = split(stage[4 + m])
        r_hi[m] = hi
        r_lo[m] = lo

    def first(i, k):
        b = (i + 1) % 8
        offset = jnp.minimum((table[0, k, b] - (blk * BLOCKS + b) + 65) % 64, 2) - 1
        item = b + offset
        item = jnp.where(item < 0, HALO_LO, item)
        lm = table[1, k, b] % 2 + 2 * k
        weight = table[3, k, b].astype(F32)
        inner = dot3(l_hi[lm], l_lo[lm], p_hi[item], p_lo[item])
        hi, lo = split(inner * weight)
        i_hi[k] = hi
        i_lo[k] = lo

    def second(i):
        b = (i + 1) % 8
        total = None
        for k in range(2):
            rm = table[2, k, b] % 2 + 2 * k
            term = dot3(i_hi[k], i_lo[k], r_hi[rm], r_lo[rm])
            total = term if total is None else total + term
        stage[i] = total

    def core_copy(i):
        return remote(
            stage.at[i, pl.ds(0, HALF)], cland.at[i], send.at[i, CORE], recv.at[i, CORE], sibling
        )

    def xa1_copy(i, d):
        return remote(
            sa.at[i, pl.ds(4 + 2 * d, 2)], xa1.at[i, d], send.at[i, XA1 + d], recv.at[i, XA1 + d],
            (x_up, x_down)[d],
        )

    def xa2_copy(i, d):
        return remote(
            sa.at[i, 2 + d], xa2.at[i, d], send.at[i, XA2 + d], recv.at[i, XA2 + d], (x_up, x_down)[d]
        )

    def ya_copy(i):
        return remote(sa.at[i, 1], ya.at[i], send.at[i, YA], recv.at[i, YA], y_other)

    def yb_copy(i):
        return remote(sb.at[i, pl.ds(8, 8)], yb.at[i], send.at[i, YB], recv.at[i, YB], y_other)

    def xb1_copy(i, d):
        return remote(
            sb.at[i, pl.ds(4 + 2 * d, 2)], xb1.at[i, d], send.at[i, XB1 + d], recv.at[i, XB1 + d],
            (x_up, x_down)[d],
        )

    def xb2_copy(i, d):
        return remote(
            sb.at[i, 2 + d], xb2.at[i, d], send.at[i, XB2 + d], recv.at[i, XB2 + d], (x_up, x_down)[d]
        )

    def out_copy(i):
        return pltpu.make_async_copy(done.at[i], out.at[(i + 1) % 8], out_sem.at[i])

    def step1(i):
        core_copy(i).wait_recv()
        for s, (dy, dx) in enumerate(ORDER):
            rows = pl.ds(s * STRIP, STRIP)
            strip = stage[i, pl.ds(HALF + s * STRIP, STRIP)] + cland[i, rows]
            sa[i, s] = strip[:, :CUT]
            for h in range(2):
                where = {(0, 0): 0, (0, 1): 1, (1, 0): 2, (1, 1): 5, (2, 0): 4, (2, 1): 6, (3, 0): 7, (3, 1): 3}
                sb[i, 8 * dy + where[dx, h]] = strip[h * 16:(h + 1) * 16, CUT:]
        yb_copy(i).start()
        xa1_copy(i, 0).start()
        xa1_copy(i, 1).start()

    def step2(i):
        for d in range(2):
            xa1_copy(i, d).wait_recv()
            sa[i, 2 + d] += xa1[i, d, 0]
            xa2_copy(i, d).start()
        yb_copy(i).wait_recv()
        sb[i, pl.ds(0, 8)] += yb[i]
        xb1_copy(i, 0).start()
        xb1_copy(i, 1).start()

    def step3(i):
        for d in range(2):
            xa2_copy(i, d).wait_recv()
        sa[i, 1] += xa1[i, 0, 1] + xa2[i, 1]
        ya_copy(i).start()
        for d in range(2):
            xb1_copy(i, d).wait_recv()
            sb[i, 2 + d] += xb1[i, d, 0]
            xb2_copy(i, d).start()

    def step4(i):
        for d in range(2):
            xb2_copy(i, d).wait_recv()
        done[i, pl.ds(0, 16), pl.ds(CUT, REST)] = sb[i, 0] + xb2[i, 0] + xb1[i, 1, 1]
        done[i, pl.ds(16, 16), pl.ds(CUT, REST)] = sb[i, 1] + xb1[i, 0, 1] + xb2[i, 1]
        ya_copy(i).wait_recv()
        done[i, :, pl.ds(0, CUT)] = (sa[i, 0] + xa2[i, 0] + xa1[i, 1, 1]) + ya[i]
        out_copy(i).start()

    steps = (step1, step2, step3, step4)

    def run_steps(i, slot):
        for step, offset in zip(steps, OFFSETS):
            if offset % 2 == slot:
                ago = offset // 2
                if isinstance(i, int):
                    if i >= ago:
                        step(i - ago)
                else:
                    @pl.when(i >= ago)
                    def _():
                        step(i - ago)

    for copy in table_loads:
        copy.wait()
    convert_left(0)
    convert_left(1)
    for j in (0, 1, 2):
        psi_load(j).wait()
        convert(j)
    first(0, 0)
    convert_left(2)
    convert_left(3)
    first(0, 1)
    pl.semaphore_wait(barrier, 6)
    halo(0).start()
    halo(1).start()
    for m in range(4):
        convert_right(m)
    second(0)
    core_copy(0).start()
    psi_load(3).wait()
    convert(3)

    def iteration(i, carry):
        first(i, 0)
        first(i, 1)
        run_steps(i, 0)

        @pl.when(i == 5)
        def _():
            halo(0).wait_recv()
            halo_pass(0).start()

        @pl.when(i == 6)
        def _():
            halo(1).wait_recv()
            halo_pass(1).start()

        second(i)
        core_copy(i).start()

        @pl.when(i < 5)
        def _():
            psi_load(i + 3).wait()

        @pl.when(i == 5)
        def _():
            halo_pass(0).wait_recv()

        @pl.when(i == 6)
        def _():
            halo_pass(1).wait_recv()

        convert(jnp.minimum(i + 3, 9))
        run_steps(i, 1)
        return carry

    lax.fori_loop(1, BLOCKS, iteration, 0)
    late = [(2 * i + off, n, i) for i in range(BLOCKS) for n, off in enumerate(OFFSETS) if 2 * i + off > 15]
    for _, n, i in sorted(late):
        steps[n](i)

    for n in range(2):
        halo(n).wait_send()
        halo_pass(n).wait_send()

    def finish(i, carry):
        core_copy(i).wait_send()
        for d in range(2):
            xa1_copy(i, d).wait_send()
            xa2_copy(i, d).wait_send()
            xb1_copy(i, d).wait_send()
            xb2_copy(i, d).wait_send()
        ya_copy(i).wait_send()
        yb_copy(i).wait_send()
        out_copy(i).wait()
        return carry

    lax.fori_loop(0, BLOCKS, finish, 0)


def body(psi, left_env, right_env, source, left_sector, right_sector, live):
    vmem = pltpu.VMEM
    dma = pltpu.SemaphoreType.DMA
    square = (WIDTH, WIDTH)
    hbm = pl.BlockSpec(memory_space=pl.ANY)
    return pl.pallas_call(
        kernel,
        out_shape=jax.ShapeDtypeStruct((BLOCKS, STRIP, WIDTH), F32),
        in_specs=[hbm] * 7,
        out_specs=hbm,
        scratch_shapes=[
            pltpu.SMEM((4, 2, BLOCKS), jnp.int32),
            vmem((8, *square), F32),
            vmem((10, *square), F32),
            vmem((10, *square), BF16),
            vmem((10, *square), BF16),
            vmem((4, *square), BF16),
            vmem((4, *square), BF16),
            vmem((4, *square), BF16),
            vmem((4, *square), BF16),
            vmem((2, *square), BF16),
            vmem((2, *square), BF16),
            vmem((8, HALF, WIDTH), F32),
            vmem((8, 8, STRIP, CUT), F32),
            vmem((8, 16, 16, REST), F32),
            vmem((8, 2, 2, STRIP, CUT), F32),
            vmem((8, 2, STRIP, CUT), F32),
            vmem((8, STRIP, CUT), F32),
            vmem((8, 8, 16, REST), F32),
            vmem((8, 2, 2, 16, REST), F32),
            vmem((8, 2, 16, REST), F32),
            vmem((8, STRIP, WIDTH), F32),
            dma((4,)), dma((8,)), dma((4,)), dma((4,)),
            dma((2,)), dma((2,)), dma((2,)), dma((2,)),
            dma((8, KINDS)), dma((8, KINDS)),
            dma((8,)),
        ],
        compiler_params=pltpu.CompilerParams(
            collective_id=0, has_side_effects=True, vmem_limit_bytes=60 * 2**20
        ),
    )(
        source.T, left_sector.T, right_sector.T, live.T, psi,
        left_env.reshape(4, *square), right_env.reshape(4, *square),
    )


def solution(mesh):
    placed = (
        P("blk", None, None),
        P("env", "blk", None, None),
        P("env", "blk", None, None),
        P("blk", "env"),
        P("blk", "env"),
        P("blk", "env"),
        P("blk", "env"),
    )
    return jax.shard_map(
        body, mesh=mesh, in_specs=placed, out_specs=P("blk", "env", None), check_vma=False
    )
```

```python
import functools

import jax
import jax.numpy as jnp
from jax import lax
from jax.experimental import pallas as pl
from jax.experimental.pallas import tpu as pltpu
from jax.sharding import PartitionSpec as P

MESH = pl.DeviceIdType.MESH
BF16 = jnp.bfloat16
F32 = jnp.float32

WIDTH = 512
BLOCKS = 8
STRIP = 32
HALF = 256
CUT = 384
REST = WIDTH - CUT
OFFSETS = (2, 7, 11, 15)
HALO_HI, HALO_LO = 8, 9
ORDER = ((0, 0), (1, 0), (0, 1), (1, 3), (0, 2), (1, 1), (1, 2), (0, 3))
CORE, XA1, XA2, YA, YB, XB1, XB2, KINDS = 0, 1, 3, 5, 6, 7, 9, 11


def split(x):
    hi = x.astype(BF16)
    return hi, (x - hi.astype(F32)).astype(BF16)


def dot3(a_hi, a_lo, b_hi, b_lo):
    dot = functools.partial(jnp.dot, preferred_element_type=F32)
    return dot(a_hi, b_hi) + dot(a_hi, b_lo) + dot(a_lo, b_hi)


def kernel(
    source, left_sector, right_sector, live, psi, left, right, out,
    table, stage, land, p_hi, p_lo, l_hi, l_lo, r_hi, r_lo, i_hi, i_lo,
    cland, sa, sb, xa1, xa2, ya, yb, xb1, xb2, done,
    table_sem, psi_sem, left_sem, right_sem, halo_send, halo_recv, pass_send, pass_recv, send, recv,
    out_sem,
):
    blk, env = lax.axis_index("blk"), lax.axis_index("env")
    core, x, y_hi = env % 2, (env // 2) % 4, env // 8

    def env_at(y, xx, c):
        return (y * 4 + xx) * 2 + c

    sibling = (blk, env_at(y_hi, x, 1 - core))
    x_up = (blk, env_at(y_hi, (x + 1) % 4, core))
    x_down = (blk, env_at(y_hi, (x + 3) % 4, core))
    y_other = (blk, env_at(1 - y_hi, x, core))
    blk_up = ((blk + 1) % 8, env)
    blk_down = ((blk + 7) % 8, env)

    def left_load(m):
        return pltpu.make_async_copy(left.at[m], stage.at[m], left_sem.at[m])

    def right_load(m):
        return pltpu.make_async_copy(right.at[m], stage.at[4 + m], right_sem.at[m])

    def psi_load(j):
        return pltpu.make_async_copy(psi.at[j], land.at[j], psi_sem.at[j])

    table_loads = [
        pltpu.make_async_copy(ref, table.at[n], table_sem.at[n])
        for n, ref in enumerate((source, left_sector, right_sector, live))
    ]
    for copy in table_loads:
        copy.start()
    for m in (0, 1):
        left_load(m).start()
    for j in (0, 1, 2):
        psi_load(j).start()
    for m in (2, 3):
        left_load(m).start()
    for m in range(4):
        right_load(m).start()
    for j in (7, 3, 4, 5, 6):
        psi_load(j).start()

    barrier = pltpu.get_barrier_semaphore()
    for peer in (sibling, x_up, x_down, y_other, blk_up, blk_down):
        pl.semaphore_signal(barrier, inc=1, device_id=peer, device_id_type=MESH)

    def remote(src, dst, s, r, peer):
        return pltpu.make_async_remote_copy(
            src_ref=src, dst_ref=dst, send_sem=s, recv_sem=r, device_id=peer, device_id_type=MESH
        )

    my_half = pl.ds(core * HALF, HALF)

    def halo(n):
        mine, theirs, peer = ((0, HALO_HI, blk_down), (7, HALO_LO, blk_up))[n]
        return remote(
            psi.at[mine, my_half], land.at[theirs, my_half], halo_send.at[n], halo_recv.at[n], peer
        )

    def halo_pass(n):
        item = (HALO_HI, HALO_LO)[n]
        return remote(
            land.at[item, my_half], land.at[item, my_half], pass_send.at[n], pass_recv.at[n], sibling
        )

    def convert(j):
        hi, lo = split(land[j])
        p_hi[j] = hi
        p_lo[j] = lo

    def convert_left(m):
        left_load(m).wait()
        for half in range(2):
            for s, (dy, dx) in enumerate(ORDER):
                owner = env_at((y_hi + dy) % 2, (x + dx) % 4, (core + 1 + half) % 2)
                hi, lo = split(stage[m, pl.ds(owner * STRIP, STRIP)])
                rows = pl.ds((half * 8 + s) * STRIP, STRIP)
                l_hi[m, rows] = hi
                l_lo[m, rows] = lo

    def convert_right(m):
        right_load(m).wait()
        hi, lo = split(stage[4 + m])
        r_hi[m] = hi
        r_lo[m] = lo

    def first(i, k):
        b = (i + 1) % 8
        offset = jnp.minimum((table[0, k, b] - (blk * BLOCKS + b) + 65) % 64, 2) - 1
        item = b + offset
        item = jnp.where(item < 0, HALO_LO, item)
        lm = table[1, k, b] % 2 + 2 * k
        weight = table[3, k, b].astype(F32)
        inner = dot3(l_hi[lm], l_lo[lm], p_hi[item], p_lo[item])
        hi, lo = split(inner * weight)
        i_hi[k] = hi
        i_lo[k] = lo

    def second(i):
        b = (i + 1) % 8
        total = None
        for k in range(2):
            rm = table[2, k, b] % 2 + 2 * k
            term = dot3(i_hi[k], i_lo[k], r_hi[rm], r_lo[rm])
            total = term if total is None else total + term
        stage[i] = total

    def core_copy(i):
        return remote(
            stage.at[i, pl.ds(0, HALF)], cland.at[i], send.at[i, CORE], recv.at[i, CORE], sibling
        )

    def xa1_copy(i, d):
        return remote(
            sa.at[i, pl.ds(4 + 2 * d, 2)], xa1.at[i, d], send.at[i, XA1 + d], recv.at[i, XA1 + d],
            (x_up, x_down)[d],
        )

    def xa2_copy(i, d):
        return remote(
            sa.at[i, 2 + d], xa2.at[i, d], send.at[i, XA2 + d], recv.at[i, XA2 + d], (x_up, x_down)[d]
        )

    def ya_copy(i):
        return remote(sa.at[i, 1], ya.at[i], send.at[i, YA], recv.at[i, YA], y_other)

    def yb_copy(i):
        return remote(sb.at[i, pl.ds(8, 8)], yb.at[i], send.at[i, YB], recv.at[i, YB], y_other)

    def xb1_copy(i, d):
        return remote(
            sb.at[i, pl.ds(4 + 2 * d, 2)], xb1.at[i, d], send.at[i, XB1 + d], recv.at[i, XB1 + d],
            (x_up, x_down)[d],
        )

    def xb2_copy(i, d):
        return remote(
            sb.at[i, 2 + d], xb2.at[i, d], send.at[i, XB2 + d], recv.at[i, XB2 + d], (x_up, x_down)[d]
        )

    def out_copy(i):
        return pltpu.make_async_copy(done.at[i], out.at[(i + 1) % 8], out_sem.at[i])

    def step1(i):
        core_copy(i).wait_recv()
        for s, (dy, dx) in enumerate(ORDER):
            rows = pl.ds(s * STRIP, STRIP)
            strip = stage[i, pl.ds(HALF + s * STRIP, STRIP)] + cland[i, rows]
            sa[i, s] = strip[:, :CUT]
            for h in range(2):
                where = {(0, 0): 0, (0, 1): 1, (1, 0): 2, (1, 1): 5, (2, 0): 4, (2, 1): 6, (3, 0): 7, (3, 1): 3}
                sb[i, 8 * dy + where[dx, h]] = strip[h * 16:(h + 1) * 16, CUT:]
        xa1_copy(i, 0).start()
        xa1_copy(i, 1).start()
        yb_copy(i).start()

    def step2(i):
        for d in range(2):
            xa1_copy(i, d).wait_recv()
            sa[i, 2 + d] += xa1[i, d, 0]
            xa2_copy(i, d).start()
        yb_copy(i).wait_recv()
        sb[i, pl.ds(0, 8)] += yb[i]
        xb1_copy(i, 0).start()
        xb1_copy(i, 1).start()

    def step3(i):
        for d in range(2):
            xa2_copy(i, d).wait_recv()
        sa[i, 1] += xa1[i, 0, 1] + xa2[i, 1]
        ya_copy(i).start()
        for d in range(2):
            xb1_copy(i, d).wait_recv()
            sb[i, 2 + d] += xb1[i, d, 0]
            xb2_copy(i, d).start()

    def step4(i):
        for d in range(2):
            xb2_copy(i, d).wait_recv()
        done[i, pl.ds(0, 16), pl.ds(CUT, REST)] = sb[i, 0] + xb2[i, 0] + xb1[i, 1, 1]
        done[i, pl.ds(16, 16), pl.ds(CUT, REST)] = sb[i, 1] + xb1[i, 0, 1] + xb2[i, 1]
        ya_copy(i).wait_recv()
        done[i, :, pl.ds(0, CUT)] = (sa[i, 0] + xa2[i, 0] + xa1[i, 1, 1]) + ya[i]
        out_copy(i).start()

    steps = (step1, step2, step3, step4)

    def run_steps(i, slot):
        for step, offset in zip(steps, OFFSETS):
            if offset % 2 == slot:
                ago = offset // 2
                if isinstance(i, int):
                    if i >= ago:
                        step(i - ago)
                else:
                    @pl.when(i >= ago)
                    def _():
                        step(i - ago)

    for copy in table_loads:
        copy.wait()
    convert_left(0)
    convert_left(1)
    for j in (0, 1, 2):
        psi_load(j).wait()
        convert(j)
    first(0, 0)
    convert_left(2)
    convert_left(3)
    first(0, 1)
    pl.semaphore_wait(barrier, 6)
    halo(0).start()
    halo(1).start()
    for m in range(4):
        convert_right(m)
    second(0)
    core_copy(0).start()
    psi_load(3).wait()
    convert(3)

    def iteration(i, carry):
        first(i, 0)
        first(i, 1)
        run_steps(i, 0)

        @pl.when(i == 5)
        def _():
            halo(0).wait_recv()
            halo_pass(0).start()

        @pl.when(i == 6)
        def _():
            halo(1).wait_recv()
            halo_pass(1).start()

        second(i)
        core_copy(i).start()

        @pl.when(i < 5)
        def _():
            psi_load(i + 3).wait()

        @pl.when(i == 5)
        def _():
            halo_pass(0).wait_recv()

        @pl.when(i == 6)
        def _():
            halo_pass(1).wait_recv()

        convert(jnp.minimum(i + 3, 9))
        run_steps(i, 1)
        return carry

    lax.fori_loop(1, BLOCKS, iteration, 0)
    late = [(2 * i + off, n, i) for i in range(BLOCKS) for n, off in enumerate(OFFSETS) if 2 * i + off > 15]
    for _, n, i in sorted(late):
        steps[n](i)

    for n in range(2):
        halo(n).wait_send()
        halo_pass(n).wait_send()

    def finish(i, carry):
        core_copy(i).wait_send()
        for d in range(2):
            xa1_copy(i, d).wait_send()
            xa2_copy(i, d).wait_send()
            xb1_copy(i, d).wait_send()
            xb2_copy(i, d).wait_send()
        ya_copy(i).wait_send()
        yb_copy(i).wait_send()
        out_copy(i).wait()
        return carry

    lax.fori_loop(0, BLOCKS, finish, 0)


def body(psi, left_env, right_env, source, left_sector, right_sector, live):
    vmem = pltpu.VMEM
    dma = pltpu.SemaphoreType.DMA
    square = (WIDTH, WIDTH)
    hbm = pl.BlockSpec(memory_space=pl.ANY)
    return pl.pallas_call(
        kernel,
        out_shape=jax.ShapeDtypeStruct((BLOCKS, STRIP, WIDTH), F32),
        in_specs=[hbm] * 7,
        out_specs=hbm,
        scratch_shapes=[
            pltpu.SMEM((4, 2, BLOCKS), jnp.int32),
            vmem((8, *square), F32),
            vmem((10, *square), F32),
            vmem((10, *square), BF16),
            vmem((10, *square), BF16),
            vmem((4, *square), BF16),
            vmem((4, *square), BF16),
            vmem((4, *square), BF16),
            vmem((4, *square), BF16),
            vmem((2, *square), BF16),
            vmem((2, *square), BF16),
            vmem((8, HALF, WIDTH), F32),
            vmem((8, 8, STRIP, CUT), F32),
            vmem((8, 16, 16, REST), F32),
            vmem((8, 2, 2, STRIP, CUT), F32),
            vmem((8, 2, STRIP, CUT), F32),
            vmem((8, STRIP, CUT), F32),
            vmem((8, 8, 16, REST), F32),
            vmem((8, 2, 2, 16, REST), F32),
            vmem((8, 2, 16, REST), F32),
            vmem((8, STRIP, WIDTH), F32),
            dma((4,)), dma((8,)), dma((4,)), dma((4,)),
            dma((2,)), dma((2,)), dma((2,)), dma((2,)),
            dma((8, KINDS)), dma((8, KINDS)),
            dma((8,)),
        ],
        compiler_params=pltpu.CompilerParams(
            collective_id=0, has_side_effects=True, vmem_limit_bytes=60 * 2**20
        ),
    )(
        source.T, left_sector.T, right_sector.T, live.T, psi,
        left_env.reshape(4, *square), right_env.reshape(4, *square),
    )


def solution(mesh):
    placed = (
        P("blk", None, None),
        P("env", "blk", None, None),
        P("env", "blk", None, None),
        P("blk", "env"),
        P("blk", "env"),
        P("blk", "env"),
        P("blk", "env"),
    )
    return jax.shard_map(
        body, mesh=mesh, in_specs=placed, out_specs=P("blk", "env", None), check_vma=False
    )
```
